32 devices in a mesh: groups: 2 (over x), lon: 16 (over z, y, core).
Axes of the slice: x: 2, y: 2, z: 4, core: 2. Of those that a mesh axis runs over, the one named last changes fastest.
Arguments:
- flux_probes: bfloat16 [768, 8, 192, 256], P('lon', 'groups'), parts along dimension 1, may hold values from -6 to 6
- time_factor: bfloat16 [192, 192], replicated, as said below
- lat_factor: bfloat16 [256, 256], replicated, as said below
- lon_factor: bfloat16 [768, 768], replicated, as said below
- footprint: bfloat16 [1024, 128, 128], P('lon'), may hold values from -0.5 to 0.5
- entry_owner: int32 [1024, 1], P('lon'), may hold values from 0 to 15; in each aligned block of 64 rows (0 to 63, 64 to 127, ...) at most 8 rows name the same one
- entry_block: int32 [1024], P('lon'), may hold values from 0 to 7
- entry_tile: int32 [1024], P('lon'), may hold values from 0 to 18431
- obs_weight: float32 [128, 128], P('lon'), may hold values from 0.1 to 1
Outputs:
- hessian_probes: bfloat16 [768, 8, 192, 256], P('lon', 'groups'), parts along dimension 1
The draws below stay inside these ranges and needn't reach their ends.
There are 2 independent parts, one for each index of `groups`. The reference program is written for one: setup_inputs(seed, part) draws one part's arguments, and reference() takes and returns one part's arrays. A program takes and returns all parts, laid end to end along the dimension named above; an argument that names none is the same for every part. Nothing has to cross between parts.
Inputs may be any that keep to these rules, and one draw needn't show every extreme that they name: `entry_owner`: on each device at most 8 of its 64 footprint tiles belong to one owner, and some owner has exactly 8. `time_factor`: lower triangular with a positive diagonal. `lat_factor`: lower triangular with a positive diagonal. `lon_factor`: lower triangular with a positive diagonal.
All inputs are finite; a program needn't handle non-finite values.
Results may differ from the reference program's by a relative error of at most 0.0034.
Values may be sent and summed in bfloat16 or wider, within the bound.
A program may use at most 192 MiB of HBM per device.

```python
import math
import jax
import jax.numpy as jnp
import numpy as np

T_SIZE = 192
LAT = 256
LON = 768
P_SIZE = 4
SND = 128
ENT_DEV = 64
BLK_DEV = 8
CAP = 8
NLB = 2
T_DEV = 12
NB = 128
EN = 1024
N_LON = 16


def lower_factor(key, order, reach, low, high):
    rows = jnp.arange(order)[:, None]
    cols = jnp.arange(order)[None, :]
    spread = jax.random.uniform(key, (order, order), jnp.float32, low, high)
    lag = jnp.maximum(rows - cols, 0).astype(jnp.float32)
    base = jnp.where(rows >= cols, jnp.exp(-lag / reach) * spread, 0.0)
    return (base * jnp.sqrt(2.0 / reach)).astype(jnp.bfloat16)


def draw_time_factor(key, part):
    key = jax.random.fold_in(key, 11)
    return lower_factor(key, T_SIZE, T_SIZE / 12.0, 0.5, 1.5)


def draw_lat_factor(key, part):
    key = jax.random.fold_in(key, 23)
    return lower_factor(key, LAT, LAT / 10.0, 0.5, 1.5)


def draw_lon_factor(key, part):
    key = jax.random.fold_in(key, 37)
    return lower_factor(key, LON, LON / 16.0, 0.5, 1.5)


def plant(result, rng, least, largest):
    extent = result.shape
    index_at = [jax.random.randint(jax.random.fold_in(rng, axis), (), 0, extent[axis]) for axis in range(len(extent))]
    result = result.at[tuple(index_at)].set(least)
    longest = extent.index(max(extent))
    index_at[longest] = (index_at[longest] + 1) % extent[longest]
    return result.at[tuple(index_at)].set(largest)


def shard_levels(stream_key, extent, pieces, low, largest):
    loudness, own = 1.0, jax.random.fold_in(stream_key, 6)
    for position, shards_of in pieces:
        heights = jnp.exp(jax.random.uniform(jax.random.fold_in(own, position), (shards_of,), jnp.float32, low / len(pieces), largest / len(pieces)))
        loudness = loudness * jnp.repeat(heights, extent[position] // shards_of).reshape([-1 if axis == position else 1 for axis in range(len(extent))])
    return loudness


def shared_out(own_key, own, number, rows, number_of, top, limit, skew):
    sequence = jax.random.permutation(own_key, number_of)
    heavy_load, common = load_shares(number_of, rows * top, limit, skew, True), load_shares(number_of, rows * top, limit, skew, False)
    places = jnp.arange(number_of)

    def named(tallies, turn):
        used = int((tallies > 0).sum())
        fixed = max(1, used // 4)
        passed = fixed + (places - fixed + turn * (used - fixed)) % max(1, number_of - fixed)
        return jnp.zeros((number_of,), jnp.int32).at[sequence[jnp.where(places < fixed, places, passed)]].set(jnp.asarray(tallies, jnp.int32))

    tallies = jnp.where(number % 4 == 0, named(heavy_load, number // 4), named(common, number - number // 4 - 1))
    mixed = jax.random.permutation(jax.random.fold_in(own, 3), number_of)
    source_of, taker = mixed[0:number_of // 2 * 2:2], mixed[1:number_of // 2 * 2:2]
    room = jnp.minimum(tallies[source_of] - 1, limit - tallies[taker]) // 2
    room = jnp.where((source_of == sequence[0]) | (taker == sequence[0]) | (tallies[taker] == 0), 0, jnp.maximum(room, 0))
    passed = jax.random.randint(jax.random.fold_in(own, 4), (number_of // 2,), 0, 1 << 20) % (room + 1)
    tallies = tallies.at[source_of].add(-passed).at[taker].add(passed)
    labels = jnp.searchsorted(jnp.cumsum(tallies), jnp.arange(rows * top), side="right").astype(jnp.int32)
    table = labels.reshape(top, rows).T
    table = table[jax.random.permutation(jax.random.fold_in(own, 1), rows)]
    turn = jax.random.randint(jax.random.fold_in(own, 2), (rows, 1), 0, top)
    return jnp.take_along_axis(table, (jnp.arange(top)[None, :] + turn) % top, axis=1)


def load_shares(count, total, most, skew, full):
    portions = [(1 << 20) // math.isqrt(grade ** skew) + 1 for grade in range(1, count + 1)]
    largest = most if full else min(most, max(-(-total // count), total * portions[0] // sum(portions)))
    least = 1 if total - largest >= count - 1 else 0
    given, rest = [largest] + [least] * (count - 1), total - largest - least * (count - 1)
    while rest > 0:
        candidates = [i for i in range(1, count) if given[i] < largest] or [i for i in range(1, count) if given[i] < most]
        whole, left = sum([portions[i] for i in candidates]), rest
        for i in candidates:
            addition = min(most - given[i], max(1, left * portions[i] // whole), rest)
            given[i] = given[i] + addition
            rest = rest - addition
    return np.array(given)


def centred(own_key, shape, width, bound, pieces=(), held_as=jnp.bfloat16):
    result = width * jax.random.normal(own_key, shape, jnp.float32)
    if pieces:
        result = result * shard_levels(own_key, shape, pieces, -0.22, 0.18)
    return jnp.clip(result, -bound, bound).astype(held_as)


def setup_inputs(seed: int = 0, part: int = 0) -> dict:
    key_list = jax.random.split(jax.random.key(seed), 10)
    part_keys = jax.random.split(jax.random.fold_in(key_list[9], part), 10)
    flux_probes = centred(part_keys[0], (LON, P_SIZE, T_SIZE, LAT), 1.0, 6.0, ((0, 16),))
    time_factor = draw_time_factor(jax.random.fold_in(key_list[9], 71), part)
    lat_factor = draw_lat_factor(jax.random.fold_in(key_list[9], 71), part)
    lon_factor = draw_lon_factor(jax.random.fold_in(key_list[9], 71), part)
    footprint = centred(key_list[4], (EN, SND, SND), SND ** -0.5, 0.5, ((0, 16),))
    entry_owner_keys = jax.random.split(jax.random.fold_in(key_list[5], 1), EN // ENT_DEV)
    entry_owner_turns = jax.random.permutation(jax.random.fold_in(key_list[5], 3), EN // ENT_DEV)
    entry_owner = jax.vmap(lambda own, number: shared_out(jax.random.fold_in(key_list[5], 2), own, number, ENT_DEV, N_LON, 1, CAP, 2))(entry_owner_keys, entry_owner_turns).reshape((EN, 1))
    entry_block = plant(jax.random.randint(key_list[6], (EN,), 0, BLK_DEV), jax.random.fold_in(key_list[6], 1), 0, BLK_DEV - 1).astype(jnp.int32)
    entry_tile = plant(jax.random.randint(key_list[7], (EN,), 0, LON * T_DEV * NLB), jax.random.fold_in(key_list[7], 1), 0, (LON * T_DEV * NLB) - 1).astype(jnp.int32)
    obs_weight = jnp.clip(jnp.exp(math.log(1.0) - 2.3025851 * jax.random.uniform(key_list[8], (NB, SND), jnp.float32) ** shard_levels(key_list[8], (NB, SND), ((0, 16),), -0.2, 0.2)), 0.1, 1.0)
    return dict(flux_probes=flux_probes, time_factor=time_factor, lat_factor=lat_factor, lon_factor=lon_factor, footprint=footprint, entry_owner=entry_owner, entry_block=entry_block, entry_tile=entry_tile, obs_weight=obs_weight)


def reference(flux_probes, time_factor, lat_factor, lon_factor, footprint, entry_owner, entry_block, entry_tile, obs_weight):
    f32 = jnp.float32
    probes = flux_probes.astype(f32)
    lat_mixed = jnp.einsum('optj,ij->opti', probes, lat_factor.astype(f32)).astype(jnp.bfloat16)
    time_mixed = jnp.einsum('ts,opsi->opti', time_factor.astype(f32), lat_mixed.astype(f32)).astype(jnp.bfloat16)
    prior_field = jnp.einsum('ko,optl->kptl', lon_factor.astype(f32), time_mixed.astype(f32)).astype(jnp.bfloat16)
    t_dev = T_SIZE // N_LON
    nlb = LAT // SND
    count = footprint.shape[0]
    holder = (jnp.arange(count) // ENT_DEV).astype(jnp.int32)
    lon_idx = entry_tile // (t_dev * nlb)
    day_idx = holder * t_dev + (entry_tile // nlb) % t_dev
    band_idx = entry_tile % nlb
    shaped = prior_field.reshape(LON, P_SIZE, T_SIZE, nlb, SND)
    tile_values = shaped[lon_idx, :, day_idx, band_idx, :]
    foot = footprint.astype(f32)
    partial_value = jnp.einsum('erc,epc->epr', foot, tile_values.astype(f32))
    global_block = entry_owner[:, 0] * BLK_DEV + entry_block
    modeled = jax.ops.segment_sum(partial_value, global_block, num_segments=BLK_DEV * N_LON)
    weighted = (obs_weight[:, None, :] * modeled).astype(jnp.bfloat16)
    back_tile = jnp.einsum('erc,epr->epc', foot, weighted[global_block].astype(f32))
    adjoint = jnp.zeros((LON, P_SIZE, T_SIZE, nlb, SND), f32).at[lon_idx, :, day_idx, band_idx, :].add(back_tile)
    adjoint_field = adjoint.reshape(LON, P_SIZE, T_SIZE, LAT).astype(jnp.bfloat16)
    lon_back = jnp.einsum('ko,kptl->optl', lon_factor.astype(f32), adjoint_field.astype(f32)).astype(jnp.bfloat16)
    time_back = jnp.einsum('ts,opti->opsi', time_factor.astype(f32), lon_back.astype(f32)).astype(jnp.bfloat16)
    lat_back = jnp.einsum('opsi,ij->opsj', time_back.astype(f32), lat_factor.astype(f32))
    return (probes + lat_back).astype(jnp.bfloat16)
```

```python
import functools

import jax
import jax.numpy as jnp
from jax import lax
from jax.experimental import pallas as pl
from jax.experimental.pallas import tpu as pltpu
from jax.sharding import PartitionSpec as P

SND = 128
GROUPS = 16
PAD = 16
f32 = jnp.float32
bf16 = jnp.bfloat16
VMEM_LIMIT = 60 * 1024 * 1024


def entry_barrier(n):
    me = lax.axis_index("lon")
    barrier = pltpu.get_barrier_semaphore()

    def greet(off, carry):
        pl.semaphore_signal(
            barrier,
            inc=1,
            device_id={"lon": lax.rem(me + off, n)},
            device_id_type=pl.DeviceIdType.MESH,
        )
        return carry

    lax.fori_loop(1, n, greet, 0)
    pl.semaphore_wait(barrier, n - 1)


def gather_kernel(n, x_ref, out_ref, send_sem, recv_sem):
    me = lax.axis_index("lon")
    entry_barrier(n)

    def push(off):
        return pltpu.make_async_remote_copy(
            src_ref=x_ref,
            dst_ref=out_ref.at[me],
            send_sem=send_sem.at[off],
            recv_sem=recv_sem.at[off],
            device_id={"lon": lax.rem(me + off, n)},
            device_id_type=pl.DeviceIdType.MESH,
        )

    def start(off, carry):
        push(off).start()
        return carry

    def finish(off, carry):
        push(off).wait()
        return carry

    lax.fori_loop(1, n, start, 0)
    out_ref[me] = x_ref[...]
    lax.fori_loop(1, n, finish, 0)


def gather(x, n, collective_id):
    return pl.pallas_call(
        functools.partial(gather_kernel, n),
        out_shape=jax.ShapeDtypeStruct((n,) + x.shape, x.dtype),
        in_specs=[pl.BlockSpec(memory_space=pltpu.VMEM)],
        out_specs=pl.BlockSpec(memory_space=pltpu.VMEM),
        scratch_shapes=[pltpu.SemaphoreType.DMA((n,)), pltpu.SemaphoreType.DMA((n,))],
        compiler_params=pltpu.CompilerParams(
            collective_id=collective_id, has_side_effects=True, vmem_limit_bytes=VMEM_LIMIT
        ),
    )(x)


def scatter_sum(n, x_ref, held, send_sem, recv_sem):
    me = lax.axis_index("lon")

    def push(off):
        peer = lax.rem(me + off, n)
        return pltpu.make_async_remote_copy(
            src_ref=x_ref.at[peer],
            dst_ref=held.at[me],
            send_sem=send_sem.at[off],
            recv_sem=recv_sem.at[off],
            device_id={"lon": peer},
            device_id_type=pl.DeviceIdType.MESH,
        )

    def start(off, carry):
        push(off).start()
        return carry

    def finish(off, total):
        push(off).wait()
        return total + held[lax.rem(me - off + n, n)]

    lax.fori_loop(1, n, start, 0)
    return finish, x_ref[me]


def reduce_kernel(n, x_ref, out_ref, held, send_sem, recv_sem):
    entry_barrier(n)
    finish, own = scatter_sum(n, x_ref, held, send_sem, recv_sem)
    out_ref[...] = own
    me = lax.axis_index("lon")

    def add(off, carry):
        out_ref[...] = finish(off, out_ref[...])
        return carry

    lax.fori_loop(1, n, add, 0)


def reduce_blocks(x, n, collective_id):
    return pl.pallas_call(
        functools.partial(reduce_kernel, n),
        out_shape=jax.ShapeDtypeStruct(x.shape[1:], x.dtype),
        in_specs=[pl.BlockSpec(memory_space=pltpu.VMEM)],
        out_specs=pl.BlockSpec(memory_space=pltpu.VMEM),
        scratch_shapes=[
            pltpu.VMEM(x.shape, x.dtype),
            pltpu.SemaphoreType.DMA((n,)),
            pltpu.SemaphoreType.DMA((n,)),
        ],
        compiler_params=pltpu.CompilerParams(
            collective_id=collective_id, has_side_effects=True, vmem_limit_bytes=VMEM_LIMIT
        ),
    )(x)


def residual_kernel(n, x_ref, w_ref, out_ref, held, mine, send_sem, recv_sem, send2, recv2):
    entry_barrier(n)
    me = lax.axis_index("lon")
    finish, own = scatter_sum(n, x_ref, held, send_sem, recv_sem)
    total = lax.fori_loop(1, n, finish, own)
    mine[...] = (w_ref[...] * total).astype(bf16).astype(f32)

    def push(off):
        return pltpu.make_async_remote_copy(
            src_ref=mine,
            dst_ref=out_ref.at[me],
            send_sem=send2.at[off],
            recv_sem=recv2.at[off],
            device_id={"lon": lax.rem(me + off, n)},
            device_id_type=pl.DeviceIdType.MESH,
        )

    def start(off, carry):
        push(off).start()
        return carry

    def done(off, carry):
        push(off).wait()
        return carry

    lax.fori_loop(1, n, start, 0)
    out_ref[me] = mine[...]
    lax.fori_loop(1, n, done, 0)


def residuals(x, weights, n, collective_id):
    sems = [pltpu.SemaphoreType.DMA((n,))] * 4
    return pl.pallas_call(
        functools.partial(residual_kernel, n),
        out_shape=jax.ShapeDtypeStruct(x.shape, x.dtype),
        in_specs=[pl.BlockSpec(memory_space=pltpu.VMEM)] * 2,
        out_specs=pl.BlockSpec(memory_space=pltpu.VMEM),
        scratch_shapes=[pltpu.VMEM(x.shape, x.dtype), pltpu.VMEM(x.shape[1:], x.dtype)] + sems,
        compiler_params=pltpu.CompilerParams(
            collective_id=collective_id, has_side_effects=True, vmem_limit_bytes=VMEM_LIMIT
        ),
    )(x, weights)


def forward_kernel(flux_ref, time_ref, sel_ref, lat_ref, band_ref, out_ref, mixed, total):
    chunk, probes, days, lats = flux_ref.shape
    tiles = band_ref.shape[1]
    step = pl.program_id(0)

    @pl.when(step == 0)
    def _():
        total[...] = jnp.zeros_like(total)

    def mix(o, carry):
        rows = pl.ds(pl.multiple_of(o * PAD, PAD), PAD)
        for p in range(probes):
            t = jnp.dot(time_ref[...], flux_ref[o, p], preferred_element_type=f32)
            mixed[p, :, rows, :] = t.astype(bf16).reshape(GROUPS, PAD, lats)
        return carry

    lax.fori_loop(0, chunk, mix, 0)

    def pick(g, carry):
        for p in range(probes):
            total[g, p] += jnp.dot(sel_ref[g], mixed[p, g], preferred_element_type=f32)
        return carry

    lax.fori_loop(0, GROUPS, pick, 0)

    @pl.when(step == pl.num_programs(0) - 1)
    def _():
        def last(g, carry):
            upper = jnp.broadcast_to(band_ref[g], (tiles, SND)) > 0
            for p in range(probes):
                z = jnp.dot(total[g, p].astype(bf16), lat_ref[...], preferred_element_type=f32)
                out_ref[g, :, p * SND : (p + 1) * SND] = jnp.where(upper, z[:, SND:], z[:, :SND])
            return carry

        lax.fori_loop(0, GROUPS, last, 0)


def backward_kernel(flux_ref, time_ref, sel_ref, back_ref, out_ref, mixed):
    chunk, probes, days, lats = flux_ref.shape

    def spread(g, carry):
        for p in range(probes):
            mixed[p, g] = jnp.dot(
                sel_ref[g], back_ref[p, g], preferred_element_type=f32
            ).astype(bf16)
        return carry

    lax.fori_loop(0, GROUPS, spread, 0)

    def mix(o, carry):
        rows = pl.ds(pl.multiple_of(o * PAD, PAD), PAD)
        for p in range(probes):
            held = mixed[p, :, rows, :].reshape(GROUPS * PAD, lats)
            t = jnp.dot(time_ref[...], held, preferred_element_type=f32)
            out_ref[o, p] = (flux_ref[o, p].astype(f32) + t).astype(bf16)
        return carry

    lax.fori_loop(0, chunk, mix, 0)


def body(
    flux_probes,
    time_factor,
    lat_factor,
    lon_factor,
    footprint,
    entry_owner,
    entry_block,
    entry_tile,
    obs_weight,
):
    n = lax.axis_size("lon")
    me = lax.axis_index("lon")
    lon_dev, probes, days, lats = flux_probes.shape
    longitudes = lon_factor.shape[0]
    bands = lats // SND
    day_dev = days // n
    blocks_dev = obs_weight.shape[0]
    entries = entry_tile.shape[0]
    tiles = entries * n // GROUPS
    span = days // GROUPS
    chunk = max(c for c in range(1, 17) if lon_dev % c == 0)

    padded = jnp.pad(entry_tile[None, :], ((0, 7), (0, -entries % 128)))
    tile_all = gather(padded, n, 0)[:, 0, :entries]
    day = jnp.arange(n, dtype=jnp.int32)[:, None] * day_dev + tile_all // bands % day_dev
    lon_of = (tile_all // (day_dev * bands)).reshape(GROUPS, tiles)
    slot = (day % span).reshape(GROUPS, tiles)
    band_of = (tile_all % bands).reshape(GROUPS, tiles)

    time_pad = jnp.pad(
        time_factor.reshape(GROUPS, span, days), ((0, 0), (0, PAD - span), (0, 0))
    ).reshape(GROUPS * PAD, days)

    wide = lon_dev * PAD
    columns = lax.dynamic_slice_in_dim(lon_factor, me * lon_dev, lon_dev, axis=1)
    repeat = (
        jnp.arange(lon_dev, dtype=jnp.int32)[:, None]
        == jnp.arange(wide, dtype=jnp.int32)[None, :] // PAD
    ).astype(bf16)
    lon_wide = jnp.dot(columns, repeat, preferred_element_type=f32).astype(bf16)
    hot = (lon_of[:, :, None] == jnp.arange(longitudes, dtype=jnp.int32)).astype(bf16)
    row_slot = jnp.arange(wide, dtype=jnp.int32) % PAD
    sel = jnp.einsum("gek,kr->ger", hot, lon_wide, preferred_element_type=f32)
    sel = jnp.where(slot[:, :, None] == row_slot, sel, 0.0).astype(bf16)
    sel_t = jnp.einsum("kr,gek->gre", lon_wide, hot, preferred_element_type=f32)
    sel_t = jnp.where(slot[:, None, :] == row_slot[None, :, None], sel_t, 0.0).astype(bf16)

    steps = lon_dev // chunk
    flux_spec = pl.BlockSpec((chunk, probes, days, lats), lambda i: (i, 0, 0, 0))
    mixed_shape = pltpu.VMEM((probes, GROUPS, chunk * PAD, lats), bf16)
    share = pl.pallas_call(
        forward_kernel,
        grid=(steps,),
        out_shape=jax.ShapeDtypeStruct((GROUPS, tiles, probes * SND), f32),
        in_specs=[
            flux_spec,
            pl.BlockSpec((GROUPS * PAD, days), lambda i: (0, 0)),
            pl.BlockSpec((GROUPS, tiles, chunk * PAD), lambda i: (0, 0, i)),
            pl.BlockSpec((lats, lats), lambda i: (0, 0)),
            pl.BlockSpec((GROUPS, tiles, 1), lambda i: (0, 0, 0)),
        ],
        out_specs=pl.BlockSpec((GROUPS, tiles, probes * SND), lambda i: (0, 0, 0)),
        scratch_shapes=[mixed_shape, pltpu.VMEM((GROUPS, probes, tiles, lats), f32)],
        compiler_params=pltpu.CompilerParams(vmem_limit_bytes=VMEM_LIMIT),
    )(flux_probes, time_pad, sel, lat_factor.T, band_of[:, :, None])

    values = reduce_blocks(share.reshape(n, entries, probes * SND), n, 1)
    tile_values = values.astype(bf16).reshape(entries, probes, SND)
    partial = jnp.einsum("erc,epc->epr", footprint, tile_values, preferred_element_type=f32)
    block = entry_owner[:, 0] * blocks_dev + entry_block
    named = jnp.arange(n * blocks_dev, dtype=jnp.int32)[:, None] == block[None, :]
    sums = jnp.dot(
        named.astype(f32),
        partial.reshape(entries, probes * SND),
        precision=lax.Precision.HIGHEST,
        preferred_element_type=f32,
    )
    weights = jnp.tile(obs_weight, (1, probes))
    weighted = residuals(sums.reshape(n, blocks_dev, probes * SND), weights, n, 2)
    weighted = weighted.reshape(n * blocks_dev, probes * SND).astype(bf16)
    resid = jnp.einsum("be,bx->ex", named.astype(bf16), weighted, preferred_element_type=f32)
    resid = resid.astype(bf16).reshape(entries, probes, SND)
    back = jnp.einsum("erc,epr->epc", footprint, resid, preferred_element_type=f32)
    back = back.astype(bf16).reshape(entries, probes * SND)
    back_all = gather(back, n, 3).reshape(GROUPS, tiles, probes, SND)
    placed = jnp.concatenate(
        [jnp.where(band_of[:, :, None, None] == b, back_all, 0) for b in range(bands)], axis=-1
    )
    back_lat = jnp.einsum(
        "gepi,ij->pgej", placed, lat_factor, preferred_element_type=f32
    ).astype(bf16)

    return pl.pallas_call(
        backward_kernel,
        grid=(steps,),
        out_shape=jax.ShapeDtypeStruct(flux_probes.shape, bf16),
        in_specs=[
            flux_spec,
            pl.BlockSpec((days, GROUPS * PAD), lambda i: (0, 0)),
            pl.BlockSpec((GROUPS, chunk * PAD, tiles), lambda i: (0, i, 0)),
            pl.BlockSpec((probes, GROUPS, tiles, lats), lambda i: (0, 0, 0, 0)),
        ],
        out_specs=flux_spec,
        scratch_shapes=[mixed_shape],
        compiler_params=pltpu.CompilerParams(vmem_limit_bytes=VMEM_LIMIT),
    )(flux_probes, time_pad.T, sel_t, back_lat)


def solution(mesh):
    in_specs = (
        P("lon", "groups", None, None),
        P(),
        P(),
        P(),
        P("lon", None, None),
        P("lon", None),
        P("lon"),
        P("lon"),
        P("lon", None),
    )
    out_specs = P("lon", "groups", None, None)
    return jax.shard_map(body, mesh=mesh, in_specs=in_specs, out_specs=out_specs, check_vma=False)
```

```python
import functools

import jax
import jax.numpy as jnp
from jax import lax
from jax.experimental import pallas as pl
from jax.experimental.pallas import tpu as pltpu
from jax.sharding import PartitionSpec as P

SND = 128
GROUPS = 16
PAD = 16
f32 = jnp.float32
bf16 = jnp.bfloat16
VMEM_LIMIT = 60 * 1024 * 1024


def entry_barrier(n):
    me = lax.axis_index("lon")
    barrier = pltpu.get_barrier_semaphore()

    def greet(off, carry):
        pl.semaphore_signal(
            barrier,
            inc=1,
            device_id={"lon": lax.rem(me + off, n)},
            device_id_type=pl.DeviceIdType.MESH,
        )
        return carry

    lax.fori_loop(1, n, greet, 0)
    pl.semaphore_wait(barrier, n - 1)


def gather_kernel(n, x_ref, out_ref, send_sem, recv_sem):
    me = lax.axis_index("lon")
    entry_barrier(n)

    def push(off):
        return pltpu.make_async_remote_copy(
            src_ref=x_ref,
            dst_ref=out_ref.at[me],
            send_sem=send_sem.at[off],
            recv_sem=recv_sem.at[off],
            device_id={"lon": lax.rem(me + off, n)},
            device_id_type=pl.DeviceIdType.MESH,
        )

    def start(off, carry):
        push(off).start()
        return carry

    def finish(off, carry):
        push(off).wait()
        return carry

    lax.fori_loop(1, n, start, 0)
    out_ref[me] = x_ref[...]
    lax.fori_loop(1, n, finish, 0)


def gather(x, n, collective_id):
    return pl.pallas_call(
        functools.partial(gather_kernel, n),
        out_shape=jax.ShapeDtypeStruct((n,) + x.shape, x.dtype),
        in_specs=[pl.BlockSpec(memory_space=pltpu.VMEM)],
        out_specs=pl.BlockSpec(memory_space=pltpu.VMEM),
        scratch_shapes=[pltpu.SemaphoreType.DMA((n,)), pltpu.SemaphoreType.DMA((n,))],
        compiler_params=pltpu.CompilerParams(
            collective_id=collective_id, has_side_effects=True, vmem_limit_bytes=VMEM_LIMIT
        ),
    )(x)


def scatter_sum(n, x_ref, held, send_sem, recv_sem):
    me = lax.axis_index("lon")

    def push(off):
        peer = lax.rem(me + off, n)
        return pltpu.make_async_remote_copy(
            src_ref=x_ref.at[peer],
            dst_ref=held.at[me],
            send_sem=send_sem.at[off],
            recv_sem=recv_sem.at[off],
            device_id={"lon": peer},
            device_id_type=pl.DeviceIdType.MESH,
        )

    def start(off, carry):
        push(off).start()
        return carry

    def finish(off, total):
        push(off).wait()
        return total + held[lax.rem(me - off + n, n)].astype(f32)

    lax.fori_loop(1, n, start, 0)
    return finish, x_ref[me].astype(f32)


def reduce_kernel(n, x_ref, out_ref, held, send_sem, recv_sem):
    entry_barrier(n)
    finish, own = scatter_sum(n, x_ref, held, send_sem, recv_sem)
    out_ref[...] = own
    me = lax.axis_index("lon")

    def add(off, carry):
        out_ref[...] = finish(off, out_ref[...])
        return carry

    lax.fori_loop(1, n, add, 0)


def reduce_blocks(x, n, collective_id):
    return pl.pallas_call(
        functools.partial(reduce_kernel, n),
        out_shape=jax.ShapeDtypeStruct(x.shape[1:], f32),
        in_specs=[pl.BlockSpec(memory_space=pltpu.VMEM)],
        out_specs=pl.BlockSpec(memory_space=pltpu.VMEM),
        scratch_shapes=[
            pltpu.VMEM(x.shape, x.dtype),
            pltpu.SemaphoreType.DMA((n,)),
            pltpu.SemaphoreType.DMA((n,)),
        ],
        compiler_params=pltpu.CompilerParams(
            collective_id=collective_id, has_side_effects=True, vmem_limit_bytes=VMEM_LIMIT
        ),
    )(x)


def residual_kernel(n, x_ref, w_ref, out_ref, held, mine, send_sem, recv_sem, send2, recv2):
    entry_barrier(n)
    me = lax.axis_index("lon")
    finish, own = scatter_sum(n, x_ref, held, send_sem, recv_sem)
    total = lax.fori_loop(1, n, finish, own)
    mine[...] = (w_ref[...] * total).astype(bf16).astype(f32)

    def push(off):
        return pltpu.make_async_remote_copy(
            src_ref=mine,
            dst_ref=out_ref.at[me],
            send_sem=send2.at[off],
            recv_sem=recv2.at[off],
            device_id={"lon": lax.rem(me + off, n)},
            device_id_type=pl.DeviceIdType.MESH,
        )

    def start(off, carry):
        push(off).start()
        return carry

    def done(off, carry):
        push(off).wait()
        return carry

    lax.fori_loop(1, n, start, 0)
    out_ref[me] = mine[...]
    lax.fori_loop(1, n, done, 0)


def residuals(x, weights, n, collective_id):
    sems = [pltpu.SemaphoreType.DMA((n,))] * 4
    return pl.pallas_call(
        functools.partial(residual_kernel, n),
        out_shape=jax.ShapeDtypeStruct(x.shape, x.dtype),
        in_specs=[pl.BlockSpec(memory_space=pltpu.VMEM)] * 2,
        out_specs=pl.BlockSpec(memory_space=pltpu.VMEM),
        scratch_shapes=[pltpu.VMEM(x.shape, x.dtype), pltpu.VMEM(x.shape[1:], x.dtype)] + sems,
        compiler_params=pltpu.CompilerParams(
            collective_id=collective_id, has_side_effects=True, vmem_limit_bytes=VMEM_LIMIT
        ),
    )(x, weights)


def repeat(count, probes, step):
    width = max(w for w in range(1, 5) if count % w == 0)

    def several(i, carry):
        for q in range(width):
            for p in range(probes):
                step(i * width + q, p)
        return carry

    lax.fori_loop(0, count // width, several, 0)


def forward_kernel(flux_ref, time_ref, sel_ref, lat_ref, band_ref, out_ref, mixed, total):
    chunk, probes, days, lats = flux_ref.shape
    tiles = band_ref.shape[1]
    step = pl.program_id(0)

    @pl.when(step == 0)
    def _():
        total[...] = jnp.zeros_like(total)

    def mix(o, p):
        rows = pl.ds(pl.multiple_of(o * PAD, PAD), PAD)
        t = jnp.dot(time_ref[...], flux_ref[o, p], preferred_element_type=f32)
        mixed[p, :, rows, :] = t.astype(bf16).reshape(GROUPS, PAD, lats)

    repeat(chunk, probes, mix)

    def pick(g, p):
        total[g, p] += jnp.dot(sel_ref[g], mixed[p, g], preferred_element_type=f32)

    repeat(GROUPS, probes, pick)

    @pl.when(step == pl.num_programs(0) - 1)
    def _():
        def last(g, carry):
            upper = jnp.broadcast_to(band_ref[g], (tiles, SND)) > 0
            for p in range(probes):
                z = jnp.dot(total[g, p].astype(bf16), lat_ref[...], preferred_element_type=f32)
                half = jnp.where(upper, z[:, SND:], z[:, :SND])
                out_ref[g, :, p * SND : (p + 1) * SND] = half.astype(bf16)
            return carry

        lax.fori_loop(0, GROUPS, last, 0)


def backward_kernel(flux_ref, time_ref, sel_ref, back_ref, out_ref, mixed):
    chunk, probes, days, lats = flux_ref.shape

    def spread(g, carry):
        turned = jnp.transpose(sel_ref[g])
        for p in range(probes):
            mixed[p, g] = jnp.dot(
                turned, back_ref[p, g], preferred_element_type=f32
            ).astype(bf16)
        return carry

    lax.fori_loop(0, GROUPS, spread, 0)

    def mix(o, p):
        rows = pl.ds(pl.multiple_of(o * PAD, PAD), PAD)
        held = mixed[p, :, rows, :].reshape(GROUPS * PAD, lats)
        t = jnp.dot(time_ref[...], held, preferred_element_type=f32)
        out_ref[o, p] = (flux_ref[o, p].astype(f32) + t).astype(bf16)

    repeat(chunk, probes, mix)


def body(
    flux_probes,
    time_factor,
    lat_factor,
    lon_factor,
    footprint,
    entry_owner,
    entry_block,
    entry_tile,
    obs_weight,
):
    n = lax.axis_size("lon")
    me = lax.axis_index("lon")
    lon_dev, probes, days, lats = flux_probes.shape
    longitudes = lon_factor.shape[0]
    bands = lats // SND
    day_dev = days // n
    blocks_dev = obs_weight.shape[0]
    entries = entry_tile.shape[0]
    tiles = entries * n // GROUPS
    span = days // GROUPS
    chunk = max(c for c in range(1, 17) if lon_dev % c == 0)

    padded = jnp.pad(entry_tile[None, :], ((0, 7), (0, -entries % 128)))
    tile_all = gather(padded, n, 0)[:, 0, :entries]
    day = jnp.arange(n, dtype=jnp.int32)[:, None] * day_dev + tile_all // bands % day_dev
    lon_of = (tile_all // (day_dev * bands)).reshape(GROUPS, tiles)
    slot = (day % span).reshape(GROUPS, tiles)
    band_of = (tile_all % bands).reshape(GROUPS, tiles)

    time_pad = jnp.pad(
        time_factor.reshape(GROUPS, span, days), ((0, 0), (0, PAD - span), (0, 0))
    ).reshape(GROUPS * PAD, days)

    wide = lon_dev * PAD
    columns = lax.dynamic_slice_in_dim(lon_factor, me * lon_dev, lon_dev, axis=1)
    repeat = (
        jnp.arange(lon_dev, dtype=jnp.int32)[:, None]
        == jnp.arange(wide, dtype=jnp.int32)[None, :] // PAD
    ).astype(bf16)
    lon_wide = jnp.dot(columns, repeat, preferred_element_type=f32).astype(bf16)
    hot = (lon_of[:, :, None] == jnp.arange(longitudes, dtype=jnp.int32)).astype(bf16)
    row_slot = jnp.arange(wide, dtype=jnp.int32) % PAD
    sel = jnp.einsum("gek,kr->ger", hot, lon_wide, preferred_element_type=f32)
    sel = jnp.where(slot[:, :, None] == row_slot, sel, 0.0).astype(bf16)

    steps = lon_dev // chunk
    flux_spec = pl.BlockSpec((chunk, probes, days, lats), lambda i: (i, 0, 0, 0))
    mixed_shape = pltpu.VMEM((probes, GROUPS, chunk * PAD, lats), bf16)
    share = pl.pallas_call(
        forward_kernel,
        grid=(steps,),
        out_shape=jax.ShapeDtypeStruct((GROUPS, tiles, probes * SND), bf16),
        in_specs=[
            flux_spec,
            pl.BlockSpec((GROUPS * PAD, days), lambda i: (0, 0)),
            pl.BlockSpec((GROUPS, tiles, chunk * PAD), lambda i: (0, 0, i)),
            pl.BlockSpec((lats, lats), lambda i: (0, 0)),
            pl.BlockSpec((GROUPS, tiles, 1), lambda i: (0, 0, 0)),
        ],
        out_specs=pl.BlockSpec((GROUPS, tiles, probes * SND), lambda i: (0, 0, 0)),
        scratch_shapes=[mixed_shape, pltpu.VMEM((GROUPS, probes, tiles, lats), f32)],
        compiler_params=pltpu.CompilerParams(vmem_limit_bytes=VMEM_LIMIT),
    )(flux_probes, time_pad, sel, lat_factor.T, band_of[:, :, None])

    values = reduce_blocks(share.reshape(n, entries, probes * SND), n, 1)
    tile_values = values.astype(bf16).reshape(entries, probes, SND)
    partial = jnp.einsum("erc,epc->epr", footprint, tile_values, preferred_element_type=f32)
    block = entry_owner[:, 0] * blocks_dev + entry_block
    named = jnp.arange(n * blocks_dev, dtype=jnp.int32)[:, None] == block[None, :]
    sums = jnp.dot(
        named.astype(f32),
        partial.reshape(entries, probes * SND),
        precision=lax.Precision.HIGHEST,
        preferred_element_type=f32,
    )
    weights = jnp.tile(obs_weight, (1, probes))
    weighted = residuals(sums.reshape(n, blocks_dev, probes * SND), weights, n, 2)
    weighted = weighted.reshape(n * blocks_dev, probes * SND).astype(bf16)
    resid = jnp.einsum("be,bx->ex", named.astype(bf16), weighted, preferred_element_type=f32)
    resid = resid.astype(bf16).reshape(entries, probes, SND)
    back = jnp.einsum("erc,epr->epc", footprint, resid, preferred_element_type=f32)
    back = back.astype(bf16).reshape(entries, probes * SND)
    back_all = gather(back, n, 3).reshape(GROUPS, tiles, probes, SND)
    placed = jnp.concatenate(
        [jnp.where(band_of[:, :, None, None] == b, back_all, 0) for b in range(bands)], axis=-1
    )
    back_lat = jnp.einsum(
        "gepi,ij->pgej", placed, lat_factor, preferred_element_type=f32
    ).astype(bf16)

    return pl.pallas_call(
        backward_kernel,
        grid=(steps,),
        out_shape=jax.ShapeDtypeStruct(flux_probes.shape, bf16),
        in_specs=[
            flux_spec,
            pl.BlockSpec((days, GROUPS * PAD), lambda i: (0, 0)),
            pl.BlockSpec((GROUPS, tiles, chunk * PAD), lambda i: (0, 0, i)),
            pl.BlockSpec((probes, GROUPS, tiles, lats), lambda i: (0, 0, 0, 0)),
        ],
        out_specs=flux_spec,
        scratch_shapes=[mixed_shape],
        compiler_params=pltpu.CompilerParams(vmem_limit_bytes=VMEM_LIMIT),
    )(flux_probes, time_pad.T, sel, back_lat)


def solution(mesh):
    in_specs = (
        P("lon", "groups", None, None),
        P(),
        P(),
        P(),
        P("lon", None, None),
        P("lon", None),
        P("lon"),
        P("lon"),
        P("lon", None),
    )
    out_specs = P("lon", "groups", None, None)
    return jax.shard_map(body, mesh=mesh, in_specs=in_specs, out_specs=out_specs, check_vma=False)
```
